32 devices in a mesh: grp: 4 (over y, core), mem: 8 (over z, x).
Axes of the slice: x: 2, y: 2, z: 4, core: 2. Of those that a mesh axis runs over, the one named last changes fastest.
Arguments:
- coefficients: float32 [8, 240, 4096], P(None, None, ('grp', 'mem')), may hold values from -6 to 6
- incident: float32 [8, 240, 4096], P(None, None, ('grp', 'mem')), may hold values from -6 to 6
- mie_coeffs: float32 [2, 240], replicated, may hold values from -0.8 to 0.8
- rot_table: bfloat16 [8, 240, 240], replicated, may hold values from -0.375 to 0.375
- axial_shells: bfloat16 [3, 2, 240, 240], replicated, may hold values from -0.1875 to 0.1875
- up_axial: bfloat16 [2, 240, 240], replicated, may hold values from -0.1875 to 0.1875
- far_axial: bfloat16 [2, 240, 240], replicated, may hold values from -0.0625 to 0.0625
- coupling: float32 [64, 64], replicated, may hold values from 0.01 to 0.1
- cluster_ids: int32 [4096], P(('grp', 'mem')), may hold values from 0 to 15
- center_rot: int32 [4096], P(('grp', 'mem')), may hold values from 0 to 7
- pair_col: int32 [24, 4096], P(None, ('grp', 'mem')), may hold values from -1 to 1407, as said below
- pair_rot: int32 [24, 4096], P(None, ('grp', 'mem')), may hold values from -1 to 7, as said below
- send_col: int32 [192, 64], P(('grp', 'mem')), may hold values from 0 to 1023, as said below
Outputs:
- updated: float32 [8, 240, 4096], P(None, None, ('grp', 'mem'))
The draws below stay inside these ranges and needn't reach their ends.
Inputs may be any that keep to these rules, and one draw needn't show every extreme that they name: `pair_col`: -1 marks an empty slot; a value below 1024 is r * 128 + j for the own device's sphere j rotated by entry r; a larger one is 1024 + p * 64 + c for the c-th column sent to this device by its neighbour p; every such received column is named by some slot of the receiving device. `pair_rot`: -1 exactly in empty slots; otherwise the table entry with which the slot's column was rotated. `send_col`: row d * 6 + p lists the pool columns r * 128 + j that device d provides to the device whose neighbour p it is.
All inputs are finite; a program needn't handle non-finite values.
Results may differ from the reference program's by a relative error of at most 0.0038.
The reference program's roundings to bfloat16 on the way count: a program that leaves them out, or rounds other values in their place, can miss the bound.
Values may be sent and summed in bfloat16 or wider, within the bound.
A program may use at most 128 MiB of HBM per device.

```python
import math
import jax
import jax.numpy as jnp
import numpy as np
from jax import lax

NCO = 240
NDIR = 4
NROT = 8
NSHELL = 3
SLOT = 8
NPEER = 6
SPH_DEV = 128
CAP = 64
NEAR = 24
NSPH = 4096
CL_GRP = 16
NCLUS = 64
N_GRP = 4
N_MEM = 8


def pair_tables(key):
    dev_count = NSPH // SPH_DEV
    pool_size = NROT * SPH_DEV
    recv_size = NPEER * CAP
    slot_count = NEAR * SPH_DEV
    base_key = jax.random.fold_in(key, 7013)
    sender = jax.random.randint(jax.random.fold_in(base_key, 1), (dev_count, NPEER, CAP), 0, pool_size, dtype=jnp.int32)
    dev_keys = jax.random.split(jax.random.fold_in(base_key, 2), dev_count)
    mem_steps = jnp.array([1, -1, 2, -2, 0, 0], dtype=jnp.int32)
    grp_steps = jnp.array([0, 0, 0, 0, 1, -1], dtype=jnp.int32)
    peer_iota = jnp.arange(NPEER, dtype=jnp.int32)

    def one_device(dev_key, target):
        grp_idx = target // N_MEM
        mem_idx = target % N_MEM
        sources = (grp_idx - grp_steps) % N_GRP * N_MEM + (mem_idx - mem_steps) % N_MEM
        ordering = jax.random.permutation(jax.random.fold_in(dev_key, 1), slot_count)
        ranking = jnp.argsort(ordering).astype(jnp.int32)
        alive = jax.random.randint(jax.random.fold_in(dev_key, 2), (slot_count,), 0, 2, dtype=jnp.int32)
        own_cols = jax.random.randint(jax.random.fold_in(dev_key, 3), (slot_count,), 0, pool_size, dtype=jnp.int32)
        incoming = sender[sources, peer_iota].reshape(-1)
        is_recv = ranking < recv_size
        rank_clip = jnp.minimum(ranking, recv_size - 1)
        col_vals = jnp.where(is_recv, pool_size + ranking, jnp.where(alive == 1, own_cols, -1))
        rot_vals = jnp.where(is_recv, incoming[rank_clip] // SPH_DEV, jnp.where(alive == 1, own_cols // SPH_DEV, -1))
        return (col_vals.reshape(NEAR, SPH_DEV), rot_vals.reshape(NEAR, SPH_DEV))
    col_table, rot_ints = jax.vmap(one_device)(dev_keys, jnp.arange(dev_count, dtype=jnp.int32))
    col_table = jnp.transpose(col_table, (1, 0, 2)).reshape(NEAR, NSPH).astype(jnp.int32)
    rot_ints = jnp.transpose(rot_ints, (1, 0, 2)).reshape(NEAR, NSPH).astype(jnp.int32)
    return (col_table, rot_ints, sender.reshape(dev_count * NPEER, CAP))


def draw_pair_col(key, part):
    return pair_tables(key)[0]


def draw_pair_rot(key, part):
    return pair_tables(key)[1]


def draw_send_col(key, part):
    return pair_tables(key)[2]


def plant(values, own_key, low, high):
    longest = values.shape.index(max(values.shape))
    spots = []
    for shift in (0, 1):
        where = [jax.random.randint(jax.random.fold_in(own_key, axis), (), 0, length) for axis, length in enumerate(values.shape)]
        where[longest] = (where[longest] + shift) % values.shape[longest]
        spots.append(tuple(where))
    return values.at[spots[0]].set(low).at[spots[1]].set(high)


def level_of(key, shape, cuts, low, largest):
    level = 1.0
    for axis_at, shards_of in cuts:
        heights = jax.random.uniform(jax.random.fold_in(jax.random.fold_in(key, 6), axis_at), (shards_of,), jnp.float32, low / len(cuts), largest / len(cuts))
        level = level * jnp.repeat(jnp.exp(heights), shape[axis_at] // shards_of).reshape((-1,) + (1,) * (len(shape) - 1 - axis_at))
    return level


def cumulative_ranks(count, lean):
    weights = [(1 << 20) // math.isqrt(rank ** lean) + 1 for rank in range(1, count + 1)]
    scale = 1 + sum(weights) // (1 << 30)
    return np.cumsum(np.array([max(1, weight // scale) for weight in weights]))


def ranked_ids(own_key, extent, count, skew):
    grid = cumulative_ranks(count, skew)
    ticket = jax.random.randint(jax.random.fold_in(own_key, 1), extent, 0, int(grid[count - 1]))
    grade = jnp.searchsorted(jnp.asarray(grid, jnp.int32), ticket, side="right")
    return jax.random.permutation(jax.random.fold_in(own_key, 2), count)[grade].astype(jnp.int32)


def centred(own_key, dims, deviation, limit, cuts=(), kind=jnp.bfloat16):
    result = deviation * jax.random.normal(own_key, dims, jnp.float32)
    if cuts:
        result = result * level_of(own_key, dims, cuts, -0.22, 0.18)
    return jnp.clip(result, -limit, limit).astype(kind)


def setup_inputs(seed: int = 0) -> dict:
    keys = jax.random.split(jax.random.key(seed), 14)
    return {
        "coefficients": centred(keys[0], (2 * NDIR, NCO, NSPH), 1.0, 6.0, ((2, 32),), jnp.float32),
        "incident": centred(keys[1], (2 * NDIR, NCO, NSPH), 1.0, 6.0, ((2, 32),), jnp.float32),
        "mie_coeffs": jnp.clip(jax.random.uniform(keys[2], (2, NCO), jnp.float32, -0.8, 0.8), -0.8, 0.8),
        "rot_table": centred(keys[3], (NROT, NCO, NCO), NCO ** -0.5, 0.375),
        "axial_shells": centred(keys[4], (NSHELL, 2, NCO, NCO), (4 * NCO) ** -0.5, 0.1875),
        "up_axial": centred(keys[5], (2, NCO, NCO), (4 * NCO) ** -0.5, 0.1875),
        "far_axial": centred(keys[6], (2, NCO, NCO), (40 * NCO) ** -0.5, 0.0625),
        "coupling": jnp.clip(jnp.exp(jax.random.uniform(keys[7], (NCLUS, NCLUS), jnp.float32, math.log(0.01), math.log(0.1))), 0.01, 0.1),
        "cluster_ids": plant(ranked_ids(keys[8], (NSPH,), CL_GRP, 2), jax.random.fold_in(keys[8], 3), 0, CL_GRP - 1).astype(jnp.int32),
        "center_rot": plant(jax.random.randint(keys[9], (NSPH,), 0, NROT), jax.random.fold_in(keys[9], 1), 0, NROT - 1).astype(jnp.int32),
        "pair_col": draw_pair_col(jax.random.fold_in(keys[13], 71), 0),
        "pair_rot": draw_pair_rot(jax.random.fold_in(keys[13], 71), 0),
        "send_col": draw_send_col(jax.random.fold_in(keys[13], 71), 0),
    }


def rounded(values):
    return lax.optimization_barrier(values.astype(jnp.bfloat16))


def complex_apply(matrix_pair, columns):
    dir_count = columns.shape[0] // 2
    real_in = columns[:dir_count].astype(jnp.float32)
    imag_in = columns[dir_count:].astype(jnp.float32)
    real_mat = matrix_pair[0].astype(jnp.float32)
    imag_mat = matrix_pair[1].astype(jnp.float32)
    real_out = jnp.einsum("kc,xcn->xkn", real_mat, real_in) - jnp.einsum("kc,xcn->xkn", imag_mat, imag_in)
    imag_out = jnp.einsum("kc,xcn->xkn", real_mat, imag_in) + jnp.einsum("kc,xcn->xkn", imag_mat, real_in)
    return jnp.concatenate([real_out, imag_out], axis=0)


def neighbour_sources(device):
    mem_steps = jnp.array([1, -1, 2, -2, 0, 0], dtype=jnp.int32)
    grp_steps = jnp.array([0, 0, 0, 0, 1, -1], dtype=jnp.int32)
    grp_idx = device // N_MEM
    mem_idx = device % N_MEM
    return (((grp_idx - grp_steps) % N_GRP) * N_MEM + (mem_idx - mem_steps) % N_MEM).astype(jnp.int32)


def reference(coefficients, incident, mie_coeffs, rot_table, axial_shells, up_axial, far_axial, coupling, cluster_ids, center_rot, pair_col, pair_rot, send_col):
    comps = coefficients.shape[0]
    dev_count = NSPH // SPH_DEV
    pool_size = NROT * SPH_DEV
    table_f = rot_table.astype(jnp.float32)
    highest = lax.Precision.HIGHEST

    def rotate_device(block):
        turned = jnp.einsum("rkc,xcn->xkrn", table_f, rounded(block).astype(jnp.float32))
        return rounded(turned).reshape(comps, NCO, pool_size)

    blocks = coefficients.reshape(comps, NCO, dev_count, SPH_DEV).transpose(2, 0, 1, 3)
    rotated = lax.map(rotate_device, blocks)
    pooled = rotated.transpose(1, 2, 0, 3).reshape(comps, NCO, dev_count * pool_size)
    sphere_ids = jnp.arange(NSPH, dtype=jnp.int32)
    owners = sphere_ids // SPH_DEV
    own_pick = owners * pool_size + center_rot * SPH_DEV + sphere_ids % SPH_DEV
    lifted = complex_apply(up_axial, jnp.take(pooled, own_pick, axis=2))
    global_cluster = (owners // N_MEM) * CL_GRP + cluster_ids
    cluster_iota = jnp.arange(NCLUS, dtype=jnp.int32)
    member_table = (global_cluster[:, None] == cluster_iota[None, :]).astype(jnp.float32)
    expansions = jnp.einsum("xkn,nc->xkc", lifted, member_table, precision=highest)
    off_diag = jnp.where(cluster_iota[:, None] == cluster_iota[None, :], jnp.float32(0.0), coupling)
    reached = jnp.einsum("cd,xkd->xkc", off_diag, expansions, precision=highest)
    far_cluster = complex_apply(far_axial, rounded(reached))
    far_each = jnp.take(far_cluster, global_cluster, axis=2)
    rot_iota = jnp.arange(NROT, dtype=jnp.int32)

    def device_field(device):
        first_sphere = device * SPH_DEV
        slot_cols = lax.dynamic_slice_in_dim(pair_col, first_sphere, SPH_DEV, 1)
        slot_rots = lax.dynamic_slice_in_dim(pair_rot, first_sphere, SPH_DEV, 1)
        own_rots = lax.dynamic_slice_in_dim(center_rot, first_sphere, SPH_DEV, 0)
        far_own = lax.dynamic_slice_in_dim(far_each, first_sphere, SPH_DEV, 2)
        sources = neighbour_sources(device)
        beyond = jnp.maximum(slot_cols - pool_size, 0)
        peer = jnp.minimum(beyond // CAP, NPEER - 1)
        source = sources[peer]
        sent_col = send_col[source * NPEER + peer, beyond % CAP]
        flat_index = jnp.where(slot_cols >= pool_size, source * pool_size + sent_col, device * pool_size + jnp.maximum(slot_cols, 0))
        fetched = jnp.take(pooled, flat_index.reshape(-1), axis=2)
        fetched = jnp.where((slot_cols >= 0).reshape(-1)[None, None, :], fetched, jnp.zeros((), fetched.dtype))
        shell_cols = fetched.reshape(comps, NCO, NSHELL, SLOT * SPH_DEV)
        pieces = []
        for shell_idx in range(NSHELL):
            pieces.append(complex_apply(axial_shells[shell_idx], shell_cols[:, :, shell_idx]))
        moved = jnp.stack(pieces, axis=2).reshape(comps, NCO, NEAR, SPH_DEV)
        selector = (slot_rots[:, None, :] == rot_iota[None, :, None]).astype(jnp.float32)
        own_select = (own_rots[None, :] == rot_iota[:, None]).astype(jnp.float32)
        totals = jnp.einsum("srn,xksn->rxkn", selector, moved, precision=highest) + own_select[:, None, None, :] * far_own[None]
        return jnp.einsum("rck,rxcn->xkn", table_f, rounded(totals).astype(jnp.float32))

    fields = lax.map(device_field, jnp.arange(dev_count, dtype=jnp.int32))
    field = fields.transpose(1, 2, 0, 3).reshape(comps, NCO, NSPH)
    summed = incident + field
    dir_count = comps // 2
    real_part = summed[:dir_count]
    imag_part = summed[dir_count:]
    mie_real = mie_coeffs[0][None, :, None]
    mie_imag = mie_coeffs[1][None, :, None]
    return jnp.concatenate([mie_real * real_part - mie_imag * imag_part, mie_real * imag_part + mie_imag * real_part], axis=0)
```

```python
import functools

import jax
import jax.numpy as jnp
from jax import lax
from jax.experimental import pallas as pl
from jax.experimental.pallas import tpu as pltpu
from jax.sharding import PartitionSpec as P

F32 = jnp.float32
BF16 = jnp.bfloat16
MIB = 1 << 20


def shifted(value, axis, by):
    length = lax.axis_size(axis)
    return lax.ppermute(value, axis, [(i, (i + by) % length) for i in range(length)])


def dot_nn(a, b):
    return jnp.dot(a, b, preferred_element_type=F32)


def dot_nt(a, b):
    return lax.dot_general(a, b, (((1,), (1,)), ((), ())), preferred_element_type=F32)


def rotate_kernel(peers, width, coef_ref, rot_ref, send_ref, clus_ref, crot_ref, *rest):
    pool_ref, sums_ref = rest[0], rest[1]
    out_refs = rest[2 : 2 + peers]
    sel = rest[2 + peers]
    comps, n_coef, sph = coef_ref.shape
    rots = rot_ref.shape[0]
    pool = rots * sph
    group = sums_ref.shape[0]
    x_all = jnp.concatenate([coef_ref[x].astype(BF16) for x in range(comps)], axis=1)
    for r in range(rots):
        turned = dot_nn(rot_ref[r], x_all).astype(BF16)
        for x in range(comps):
            pool_ref[x * n_coef : (x + 1) * n_coef, r * sph : (r + 1) * sph] = turned[
                :, x * sph : (x + 1) * sph
            ]
    total = peers * width
    col_iota = lax.broadcasted_iota(jnp.int32, (total, sph), 1)
    clus_iota = lax.broadcasted_iota(jnp.int32, (group, sph), 0)
    for r in range(rots):
        hit = send_ref[...] == col_iota + r * sph
        sel[:total, r * sph : (r + 1) * sph] = jnp.where(hit, 1.0, 0.0).astype(BF16)
        own = (clus_ref[...] == clus_iota) & (crot_ref[...] == r)
        sel[total:, r * sph : (r + 1) * sph] = jnp.where(own, 1.0, 0.0).astype(BF16)
    rows = comps * n_coef
    step = 3 * sph
    for at in range(0, rows, step):
        picked = dot_nt(sel[...], pool_ref[at : at + step, :])
        for p in range(peers):
            out_refs[p][:, at : at + step] = picked[p * width : (p + 1) * width].astype(BF16)
        sums_ref[:, at : at + step] = picked[total:]


def gather_kernel(
    peers,
    per_shell,
    pool_ref,
    exp_ref,
    *rest,
):
    recv_refs = rest[:peers]
    (
        coup_ref, axial_ref, up_ref, far_ref, rott_ref, mie_ref, inc_ref,
        gid_ref, crot_ref, pcol_ref, prot_ref, out_ref,
        recv_s, count_s, sel_s, taken_s, far_s, gath_s,
    ) = rest[peers:]
    comps, n_coef, sph = inc_ref.shape
    dirs = comps // 2
    slots = pcol_ref.shape[0]
    shells = slots // per_shell
    pool = pool_ref.shape[1]
    rots = pool // sph
    width = recv_refs[0].shape[0]
    total = peers * width
    clus = coup_ref.shape[0]
    half = dirs * sph

    arrived = jnp.concatenate([recv_refs[p][...] for p in range(peers)], axis=0)
    recv_s[...] = arrived.T

    q_iota = lax.broadcasted_iota(jnp.int32, (total, sph), 0) + pool
    rot_of = jnp.full((total, sph), -1.0, F32)
    for h in range(shells):
        count = jnp.zeros((total, sph), F32)
        for s in range(h * per_shell, (h + 1) * per_shell):
            hit = pcol_ref[s : s + 1, :] == q_iota
            count = count + jnp.where(hit, 1.0, 0.0)
            rot_of = jnp.where(hit, prot_ref[s : s + 1, :].astype(F32), rot_of)
        count_s[:, h * sph : (h + 1) * sph] = count.astype(BF16)
    rot_of = jnp.max(rot_of, axis=1, keepdims=True)

    clus_iota = lax.broadcasted_iota(jnp.int32, (clus, sph), 0)
    member = jnp.where(gid_ref[...] == clus_iota, 1.0, 0.0).astype(F32)
    weights = jnp.dot(coup_ref[...], member, precision=lax.Precision.HIGHEST, preferred_element_type=F32)
    near_sum = jnp.dot(
        exp_ref[...].T, weights, precision=lax.Precision.HIGHEST, preferred_element_type=F32
    )
    folded = jnp.concatenate(
        [
            jnp.concatenate(
                [near_sum[(c * dirs + d) * n_coef : (c * dirs + d + 1) * n_coef] for d in range(dirs)],
                axis=1,
            )
            for c in range(2)
        ],
        axis=0,
    )
    high = folded.astype(BF16)
    low = (folded - high.astype(F32)).astype(BF16)
    reached = dot_nn(up_ref[...], high) + dot_nn(up_ref[...], low)
    far_s[...] = dot_nn(far_ref[...], reached.astype(BF16))

    j_iota = lax.broadcasted_iota(jnp.int32, (sph, sph), 0)

    @pl.loop(0, rots)
    def _(r):
        first = pl.multiple_of(r * sph, sph)
        ids = j_iota + r * sph
        for h in range(shells):
            count = jnp.zeros((sph, sph), F32)
            for s in range(h * per_shell, (h + 1) * per_shell):
                count = count + jnp.where(pcol_ref[s : s + 1, :] == ids, 1.0, 0.0)
            sel_s[:sph, h * sph : (h + 1) * sph] = count.astype(BF16)
        mine = rot_of == r.astype(F32)
        sel_s[sph:, :] = jnp.where(mine, count_s[...].astype(F32), 0.0).astype(BF16)
        sel = sel_s[...]
        for x in range(comps):
            c, d = x // dirs, x % dirs
            rows = slice(x * n_coef, (x + 1) * n_coef)
            lhs = jnp.concatenate([pool_ref[rows, pl.ds(first, sph)], recv_s[rows, :]], axis=1)
            taken = dot_nn(lhs, sel).astype(BF16)
            for h in range(shells):
                at = (h * 2 + c) * n_coef
                taken_s[at : at + n_coef, d * sph : (d + 1) * sph] = taken[:, h * sph : (h + 1) * sph]
        moved = dot_nn(axial_ref[...], taken_s[...])
        here = jnp.concatenate([crot_ref[...]] * dirs, axis=1) == r
        summed = (moved + jnp.where(here, far_s[...], 0.0)).astype(BF16)
        gath_s[r, :, :half] = summed[:n_coef]
        gath_s[r, :, half:] = summed[n_coef:]

    field = dot_nn(rott_ref[...], gath_s[...].reshape(rots * n_coef, comps * sph))
    mie_r = mie_ref[:, 0:1]
    mie_i = mie_ref[:, 1:2]
    for d in range(dirs):
        re = inc_ref[d] + field[:, d * sph : (d + 1) * sph]
        im = inc_ref[dirs + d] + field[:, half + d * sph : half + (d + 1) * sph]
        out_ref[d] = mie_r * re - mie_i * im
        out_ref[dirs + d] = mie_r * im + mie_i * re


def complex_block(pair):
    return jnp.concatenate(
        [
            jnp.concatenate([pair[..., 0, :, :], -pair[..., 1, :, :]], axis=-1),
            jnp.concatenate([pair[..., 1, :, :], pair[..., 0, :, :]], axis=-1),
        ],
        axis=-2,
    )


def on_device(
    coefficients,
    incident,
    mie_coeffs,
    rot_table,
    axial_shells,
    up_axial,
    far_axial,
    coupling,
    cluster_ids,
    center_rot,
    pair_col,
    pair_rot,
    send_col,
):
    comps, n_coef, sph = coefficients.shape
    rots = rot_table.shape[0]
    pool = rots * sph
    rows = comps * n_coef
    clus = coupling.shape[0]
    group = clus // lax.axis_size("grp")
    peers, width = send_col.shape
    total = peers * width
    shells = axial_shells.shape[0]
    per_shell = pair_col.shape[0] // shells
    dirs = comps // 2
    vmem = pl.BlockSpec(memory_space=pltpu.VMEM)
    clus_row = cluster_ids.reshape(1, sph)
    crot_row = center_rot.reshape(1, sph)

    first = pl.pallas_call(
        functools.partial(rotate_kernel, peers, width),
        out_shape=[
            jax.ShapeDtypeStruct((rows, pool), BF16),
            jax.ShapeDtypeStruct((group, rows), F32),
        ]
        + [jax.ShapeDtypeStruct((width, rows), BF16)] * peers,
        in_specs=[vmem] * 5,
        out_specs=[vmem] * (2 + peers),
        scratch_shapes=[pltpu.VMEM((total + group, pool), BF16)],
        compiler_params=pltpu.CompilerParams(vmem_limit_bytes=40 * MIB),
        name="rotate",
    )(coefficients, rot_table, send_col.reshape(total, 1), clus_row, crot_row)
    rotated, sums = first[0], first[1]
    outgoing = first[2:]
    shares = lax.psum_scatter(sums, "mem", scatter_dimension=0, tiled=True)
    expansions = lax.all_gather(shares, ("grp", "mem"), axis=0, tiled=True)
    mem_moves = [1, -1, 2, -2]
    grp_moves = [1, -1]
    received = [shifted(outgoing[i], "mem", by) for i, by in enumerate(mem_moves)]
    received += [
        shifted(outgoing[len(mem_moves) + i], "grp", by) for i, by in enumerate(grp_moves)
    ]

    axial = complex_block(axial_shells)
    axial = jnp.transpose(axial, (1, 0, 2)).reshape(2 * n_coef, shells * 2 * n_coef)
    up = complex_block(up_axial)
    far = complex_block(far_axial)
    rott = jnp.transpose(rot_table, (2, 0, 1)).reshape(n_coef, rots * n_coef)
    eye = jnp.arange(clus)[:, None] == jnp.arange(clus)[None, :]
    coup_t = jnp.where(eye, F32(0.0), coupling).T
    gid = clus_row + lax.axis_index("grp") * group
    half = dirs * sph
    return pl.pallas_call(
        functools.partial(gather_kernel, peers, per_shell),
        out_shape=jax.ShapeDtypeStruct((comps, n_coef, sph), F32),
        in_specs=[vmem] * (13 + peers),
        out_specs=vmem,
        scratch_shapes=[
            pltpu.VMEM((rows, total), BF16),
            pltpu.VMEM((total, shells * sph), BF16),
            pltpu.VMEM((sph + total, shells * sph), BF16),
            pltpu.VMEM((shells * 2 * n_coef, half), BF16),
            pltpu.VMEM((2 * n_coef, half), F32),
            pltpu.VMEM((rots, n_coef, comps * sph), BF16),
        ],
        compiler_params=pltpu.CompilerParams(vmem_limit_bytes=48 * MIB),
        name="gather",
    )(
        rotated, expansions, *received, coup_t, axial, up, far, rott, mie_coeffs.T, incident,
        gid, crot_row, pair_col, pair_rot,
    )


def solution(mesh):
    cut = ("grp", "mem")
    in_specs = (
        P(None, None, cut),
        P(None, None, cut),
        P(),
        P(),
        P(),
        P(),
        P(),
        P(),
        P(cut),
        P(cut),
        P(None, cut),
        P(None, cut),
        P(cut, None),
    )
    return jax.shard_map(
        on_device, mesh=mesh, in_specs=in_specs, out_specs=P(None, None, cut), check_vma=False
    )
```

```python
import functools

import jax
import jax.numpy as jnp
from jax import lax
from jax.experimental import pallas as pl
from jax.experimental.pallas import tpu as pltpu
from jax.sharding import PartitionSpec as P

F32 = jnp.float32
BF16 = jnp.bfloat16
MIB = 1 << 20


MESH = pl.DeviceIdType.MESH
MEM_MOVES = (1, -1, 2, -2)
GRP_MOVES = (1, -1)


def exchange_kernel(peers, n_grp, n_mem, *refs):
    out_refs = refs[:peers]
    sums_ref = refs[peers]
    recv_refs = refs[peers + 1 : 2 * peers + 1]
    exp_ref = refs[2 * peers + 1]
    parts, near_s, near_r, red_s, red_r, grp_s, grp_r, mem_s, mem_r = refs[2 * peers + 2 :]
    g = lax.axis_index("grp")
    m = lax.axis_index("mem")

    def mem_peer(by):
        return (g, lax.rem(m + by + n_mem, n_mem))

    def grp_peer(by):
        return (lax.rem(g + by + n_grp, n_grp), m)

    def copy(src, dst, send, recv, device):
        return pltpu.make_async_remote_copy(
            src_ref=src, dst_ref=dst, send_sem=send, recv_sem=recv,
            device_id=device, device_id_type=MESH,
        )

    everyone = [mem_peer(k) for k in range(1, n_mem)] + [grp_peer(k) for k in range(1, n_grp)]
    barrier = pltpu.get_barrier_semaphore()
    for device in everyone:
        pl.semaphore_signal(barrier, inc=1, device_id=device, device_id_type=MESH)
    pl.semaphore_wait(barrier, len(everyone))

    reduce_copies = []
    for k in range(1, n_mem):
        device = mem_peer(k)
        reduce_copies.append(
            copy(sums_ref.at[device[1]], parts.at[k - 1], red_s.at[k - 1], red_r.at[k - 1], device)
        )
    near_peers = [mem_peer(by) for by in MEM_MOVES] + [grp_peer(by) for by in GRP_MOVES]
    near_copies = [
        copy(out_refs[p], recv_refs[p], near_s.at[p], near_r.at[p], near_peers[p])
        for p in range(peers)
    ]
    for c in reduce_copies + near_copies:
        c.start()
    for c in reduce_copies:
        c.wait_recv()
    share = sums_ref[m]
    for k in range(1, n_mem):
        share = share + parts[k - 1]
    exp_ref[m, g] = share
    grp_copies = [
        copy(exp_ref.at[m, g], exp_ref.at[m, g], grp_s.at[k - 1], grp_r.at[k - 1], grp_peer(k))
        for k in range(1, n_grp)
    ]
    for c in grp_copies:
        c.start()
    for c in grp_copies:
        c.wait_recv()
    mem_copies = [
        copy(exp_ref.at[m], exp_ref.at[m], mem_s.at[k - 1], mem_r.at[k - 1], mem_peer(k))
        for k in range(1, n_mem)
    ]
    for c in mem_copies:
        c.start()
    for c in near_copies + mem_copies:
        c.wait_recv()
    for c in reduce_copies + near_copies + grp_copies + mem_copies:
        c.wait_send()


def pair_apply(pair, wide):
    n_coef = pair.shape[1]
    half = wide.shape[1] // 2
    return pair_combine(dot_nn(pair.reshape(2 * n_coef, n_coef), wide), n_coef, half)


def pair_combine(acc, n_coef, half):
    return (
        acc[:n_coef, :half] - acc[n_coef:, half:],
        acc[:n_coef, half:] + acc[n_coef:, :half],
    )


def dot_nn(a, b):
    return jnp.dot(a, b, preferred_element_type=F32)


def dot_nt(a, b):
    return lax.dot_general(a, b, (((1,), (1,)), ((), ())), preferred_element_type=F32)


def rotate_kernel(peers, width, coef_ref, rot_ref, send_ref, clus_ref, crot_ref, *rest):
    pool_ref, sums_ref = rest[0], rest[1]
    out_refs = rest[2 : 2 + peers]
    sel = rest[2 + peers]
    comps, n_coef, sph = coef_ref.shape
    rots = rot_ref.shape[0]
    pool = rots * sph
    members, each = sums_ref.shape[0], sums_ref.shape[1]
    group = members * each
    x_all = jnp.concatenate([coef_ref[x].astype(BF16) for x in range(comps)], axis=1)
    for r in range(rots):
        turned = dot_nn(rot_ref[r], x_all).astype(BF16)
        for x in range(comps):
            pool_ref[x * n_coef : (x + 1) * n_coef, r * sph : (r + 1) * sph] = turned[
                :, x * sph : (x + 1) * sph
            ]
    total = peers * width
    col_iota = lax.broadcasted_iota(jnp.int32, (total, sph), 1)
    clus_iota = lax.broadcasted_iota(jnp.int32, (group, sph), 0)
    for r in range(rots):
        hit = send_ref[...] == col_iota + r * sph
        sel[:total, r * sph : (r + 1) * sph] = jnp.where(hit, 1.0, 0.0).astype(BF16)
        own = (clus_ref[...] == clus_iota) & (crot_ref[...] == r)
        sel[total:, r * sph : (r + 1) * sph] = jnp.where(own, 1.0, 0.0).astype(BF16)
    rows = comps * n_coef
    step = 3 * sph
    for at in range(0, rows, step):
        picked = dot_nt(sel[...], pool_ref[at : at + step, :])
        for p in range(peers):
            out_refs[p][:, at : at + step] = picked[p * width : (p + 1) * width].astype(BF16)
        for q in range(members):
            row = total + q * each
            sums_ref[q, :, at : at + step] = picked[row : row + each]


def gather_kernel(
    peers,
    per_shell,
    pool_ref,
    exp_ref,
    *rest,
):
    recv_refs = rest[:peers]
    (
        coup_ref, axial_ref, up_ref, far_ref, rott_ref, mie_ref, inc_ref,
        gid_ref, crot_ref, pcol_ref, prot_ref, out_ref,
        recv_s, count_s, sel_s, taken_s, far_s, gath_s,
    ) = rest[peers:]
    comps, n_coef, sph = inc_ref.shape
    dirs = comps // 2
    slots = pcol_ref.shape[0]
    shells = slots // per_shell
    pool = pool_ref.shape[1]
    rots = pool // sph
    width = recv_refs[0].shape[0]
    total = peers * width
    clus = coup_ref.shape[0]
    half = dirs * sph

    arrived = jnp.concatenate([recv_refs[p][...] for p in range(peers)], axis=0)
    recv_s[...] = arrived.T

    q_iota = lax.broadcasted_iota(jnp.int32, (total, sph), 0) + pool
    rot_of = jnp.full((total, sph), -1.0, F32)
    for h in range(shells):
        count = jnp.zeros((total, sph), F32)
        for s in range(h * per_shell, (h + 1) * per_shell):
            hit = pcol_ref[s : s + 1, :] == q_iota
            count = count + jnp.where(hit, 1.0, 0.0)
            rot_of = jnp.where(hit, prot_ref[s : s + 1, :].astype(F32), rot_of)
        count_s[:, h * sph : (h + 1) * sph] = count.astype(BF16)
    rot_of = jnp.max(rot_of, axis=1, keepdims=True)

    clus_iota = lax.broadcasted_iota(jnp.int32, (clus, sph), 0)
    member = jnp.where(gid_ref[...] == clus_iota, 1.0, 0.0).astype(F32)
    weights = jnp.dot(coup_ref[...], member, precision=lax.Precision.HIGHEST, preferred_element_type=F32)
    near_sum = jnp.dot(
        exp_ref[...].T, weights, precision=lax.Precision.HIGHEST, preferred_element_type=F32
    )
    folded = jnp.concatenate(
        [near_sum[x * n_coef : (x + 1) * n_coef] for x in range(comps)], axis=1
    )
    high = folded.astype(BF16)
    low = (folded - high.astype(F32)).astype(BF16)
    high_re, high_im = pair_apply(up_ref[...], high)
    low_re, low_im = pair_apply(up_ref[...], low)
    reached = jnp.concatenate([high_re + low_re, high_im + low_im], axis=1).astype(BF16)
    far_re, far_im = pair_apply(far_ref[...], reached)
    far_s[:, :half] = far_re
    far_s[:, half:] = far_im

    j_iota = lax.broadcasted_iota(jnp.int32, (sph, sph), 0)

    @pl.loop(0, rots)
    def _(r):
        first = pl.multiple_of(r * sph, sph)
        ids = j_iota + r * sph
        for h in range(shells):
            count = jnp.zeros((sph, sph), F32)
            for s in range(h * per_shell, (h + 1) * per_shell):
                count = count + jnp.where(pcol_ref[s : s + 1, :] == ids, 1.0, 0.0)
            sel_s[:sph, h * sph : (h + 1) * sph] = count.astype(BF16)
        mine = rot_of == r.astype(F32)
        sel_s[sph:, :] = jnp.where(mine, count_s[...].astype(F32), 0.0).astype(BF16)
        sel = sel_s[...]
        for x in range(comps):
            rows = slice(x * n_coef, (x + 1) * n_coef)
            lhs = jnp.concatenate([pool_ref[rows, pl.ds(first, sph)], recv_s[rows, :]], axis=1)
            taken = dot_nn(lhs, sel).astype(BF16)
            for h in range(shells):
                taken_s[h, :, x * sph : (x + 1) * sph] = taken[:, h * sph : (h + 1) * sph]
        acc = dot_nn(axial_ref[0].reshape(2 * n_coef, n_coef), taken_s[0])
        for h in range(1, shells):
            acc = acc + dot_nn(axial_ref[h].reshape(2 * n_coef, n_coef), taken_s[h])
        moved_re, moved_im = pair_combine(acc, n_coef, half)
        here = jnp.concatenate([crot_ref[...]] * dirs, axis=1) == r
        gath_s[r, :, :half] = (moved_re + jnp.where(here, far_s[:, :half], 0.0)).astype(BF16)
        gath_s[r, :, half:] = (moved_im + jnp.where(here, far_s[:, half:], 0.0)).astype(BF16)

    field = dot_nn(rott_ref[...], gath_s[...].reshape(rots * n_coef, comps * sph))
    mie_r = mie_ref[:, 0:1]
    mie_i = mie_ref[:, 1:2]
    for d in range(dirs):
        re = inc_ref[d] + field[:, d * sph : (d + 1) * sph]
        im = inc_ref[dirs + d] + field[:, half + d * sph : half + (d + 1) * sph]
        out_ref[d] = mie_r * re - mie_i * im
        out_ref[dirs + d] = mie_r * im + mie_i * re


def on_device(
    coefficients,
    incident,
    mie_coeffs,
    rot_table,
    axial_shells,
    up_axial,
    far_axial,
    coupling,
    cluster_ids,
    center_rot,
    pair_col,
    pair_rot,
    send_col,
):
    comps, n_coef, sph = coefficients.shape
    rots = rot_table.shape[0]
    pool = rots * sph
    rows = comps * n_coef
    clus = coupling.shape[0]
    n_grp, n_mem = lax.axis_size("grp"), lax.axis_size("mem")
    group = clus // n_grp
    each = group // n_mem
    peers, width = send_col.shape
    total = peers * width
    shells = axial_shells.shape[0]
    per_shell = pair_col.shape[0] // shells
    vmem = pl.BlockSpec(memory_space=pltpu.VMEM)
    clus_row = cluster_ids.reshape(1, sph)
    crot_row = center_rot.reshape(1, sph)

    first = pl.pallas_call(
        functools.partial(rotate_kernel, peers, width),
        out_shape=[
            jax.ShapeDtypeStruct((rows, pool), BF16),
            jax.ShapeDtypeStruct((n_mem, each, rows), F32),
        ]
        + [jax.ShapeDtypeStruct((width, rows), BF16)] * peers,
        in_specs=[vmem] * 5,
        out_specs=[vmem] * (2 + peers),
        scratch_shapes=[pltpu.VMEM((total + group, pool), BF16)],
        compiler_params=pltpu.CompilerParams(vmem_limit_bytes=40 * MIB),
        name="rotate",
    )(coefficients, rot_table, send_col.reshape(total, 1), clus_row, crot_row)
    rotated, sums = first[0], first[1]
    outgoing = first[2:]
    dma = pltpu.SemaphoreType.DMA
    exchanged = pl.pallas_call(
        functools.partial(exchange_kernel, peers, n_grp, n_mem),
        out_shape=[jax.ShapeDtypeStruct((width, rows), BF16)] * peers
        + [jax.ShapeDtypeStruct((n_mem, n_grp, each, rows), F32)],
        in_specs=[vmem] * (peers + 1),
        out_specs=[vmem] * (peers + 1),
        scratch_shapes=[pltpu.VMEM((n_mem - 1, each, rows), F32)]
        + [dma((peers,))] * 2
        + [dma((n_mem - 1,))] * 2
        + [dma((n_grp - 1,))] * 2
        + [dma((n_mem - 1,))] * 2,
        compiler_params=pltpu.CompilerParams(
            collective_id=0, has_side_effects=True, vmem_limit_bytes=32 * MIB
        ),
        name="exchange",
    )(*outgoing, sums)
    received = exchanged[:peers]
    expansions = exchanged[peers].reshape(clus, rows)

    rott = jnp.transpose(rot_table, (2, 0, 1)).reshape(n_coef, rots * n_coef)
    eye = jnp.arange(clus)[:, None] == jnp.arange(clus)[None, :]
    coup_t = jnp.where(eye, F32(0.0), coupling).T
    coup_t = coup_t.reshape(n_grp, n_mem, each, clus).transpose(1, 0, 2, 3).reshape(clus, clus)
    gid = clus_row + lax.axis_index("grp") * group
    return pl.pallas_call(
        functools.partial(gather_kernel, peers, per_shell),
        out_shape=jax.ShapeDtypeStruct((comps, n_coef, sph), F32),
        in_specs=[vmem] * (13 + peers),
        out_specs=vmem,
        scratch_shapes=[
            pltpu.VMEM((rows, total), BF16),
            pltpu.VMEM((total, shells * sph), BF16),
            pltpu.VMEM((sph + total, shells * sph), BF16),
            pltpu.VMEM((shells, n_coef, comps * sph), BF16),
            pltpu.VMEM((n_coef, comps * sph), F32),
            pltpu.VMEM((rots, n_coef, comps * sph), BF16),
        ],
        compiler_params=pltpu.CompilerParams(vmem_limit_bytes=48 * MIB),
        name="gather",
    )(
        rotated, expansions, *received, coup_t, axial_shells, up_axial, far_axial, rott, mie_coeffs.T, incident,
        gid, crot_row, pair_col, pair_rot,
    )


def solution(mesh):
    cut = ("grp", "mem")
    in_specs = (
        P(None, None, cut),
        P(None, None, cut),
        P(),
        P(),
        P(),
        P(),
        P(),
        P(),
        P(cut),
        P(cut),
        P(None, cut),
        P(None, cut),
        P(cut, None),
    )
    return jax.shard_map(
        on_device, mesh=mesh, in_specs=in_specs, out_specs=P(None, None, cut), check_vma=False
    )
```

```python
import functools

import jax
import jax.numpy as jnp
from jax import lax
from jax.experimental import pallas as pl
from jax.experimental.pallas import tpu as pltpu
from jax.sharding import PartitionSpec as P

F32 = jnp.float32
BF16 = jnp.bfloat16
MIB = 1 << 20


MESH = pl.DeviceIdType.MESH
MEM_MOVES = (1, -1, 2, -2)
GRP_MOVES = (1, -1)


def sweep_kernel(peers, per_shell, n_grp, n_mem, *refs):
    coef_ref, rot_ref, send_ref, clus_ref = refs[:4]
    coup_ref, axial_ref, up_ref, far_ref, rott_ref, mie_ref, inc_ref = refs[4:11]
    gid_ref, crot_ref, pcol_ref, prot_ref, out_ref = refs[11:16]
    pool_ref, sums_ref, sent_ref, send_sel, got_ref, exp_ref, flat_ref = refs[16:23]
    recv_s, count_s, sel_s, taken_s, far_s, gath_s, parts = refs[23:30]
    near_s, near_r, red_s, red_r, grp_s, grp_r, mem_s, mem_r = refs[30:]
    width = sent_ref.shape[1]
    out_refs = [sent_ref.at[p] for p in range(peers)]
    recv_refs = [got_ref.at[p] for p in range(peers)]
    g = lax.axis_index("grp")
    m = lax.axis_index("mem")

    def mem_peer(by):
        return (g, lax.rem(m + by + n_mem, n_mem))

    def grp_peer(by):
        return (lax.rem(g + by + n_grp, n_grp), m)

    def copy(src, dst, send, recv, device):
        return pltpu.make_async_remote_copy(
            src_ref=src, dst_ref=dst, send_sem=send, recv_sem=recv,
            device_id=device, device_id_type=MESH,
        )

    everyone = [mem_peer(k) for k in range(1, n_mem)] + [grp_peer(k) for k in range(1, n_grp)]
    barrier = pltpu.get_barrier_semaphore()
    for device in everyone:
        pl.semaphore_signal(barrier, inc=1, device_id=device, device_id_type=MESH)
    rotate_columns(
        peers, width, coef_ref, rot_ref, send_ref, clus_ref, crot_ref,
        pool_ref, sums_ref, out_refs, send_sel,
    )
    pl.semaphore_wait(barrier, len(everyone))

    reduce_copies = []
    for k in range(1, n_mem):
        device = mem_peer(k)
        reduce_copies.append(
            copy(sums_ref.at[device[1]], parts.at[k - 1], red_s.at[k - 1], red_r.at[k - 1], device)
        )
    near_peers = [mem_peer(by) for by in MEM_MOVES] + [grp_peer(by) for by in GRP_MOVES]
    near_copies = [
        copy(out_refs[p], recv_refs[p], near_s.at[p], near_r.at[p], near_peers[p])
        for p in range(peers)
    ]
    for c in reduce_copies + near_copies:
        c.start()
    for c in reduce_copies:
        c.wait_recv()
    share = sums_ref[m]
    for k in range(1, n_mem):
        share = share + parts[k - 1]
    exp_ref[m, g] = share
    grp_copies = [
        copy(exp_ref.at[m, g], exp_ref.at[m, g], grp_s.at[k - 1], grp_r.at[k - 1], grp_peer(k))
        for k in range(1, n_grp)
    ]
    for c in grp_copies:
        c.start()
    for c in grp_copies:
        c.wait_recv()
    mem_copies = [
        copy(exp_ref.at[m], exp_ref.at[m], mem_s.at[k - 1], mem_r.at[k - 1], mem_peer(k))
        for k in range(1, n_mem)
    ]
    for c in mem_copies:
        c.start()
    rot_of = count_slots(peers, per_shell, sent_ref, pool_ref, inc_ref, pcol_ref, prot_ref, count_s, sel_s)
    for c in near_copies + mem_copies:
        c.wait_recv()
    for c in reduce_copies + near_copies + grp_copies + mem_copies:
        c.wait_send()
    gather_columns(
        peers, per_shell, rot_of, pool_ref, exp_ref, flat_ref, recv_refs,
        coup_ref, axial_ref, up_ref, far_ref, rott_ref, mie_ref, inc_ref,
        gid_ref, crot_ref, pcol_ref, out_ref,
        recv_s, count_s, sel_s, taken_s, far_s, gath_s,
    )


def pair_apply(pair, wide):
    n_coef = pair.shape[1]
    half = wide.shape[1] // 2
    return pair_combine(dot_nn(pair.reshape(2 * n_coef, n_coef), wide), n_coef, half)


def pair_combine(acc, n_coef, half):
    return (
        acc[:n_coef, :half] - acc[n_coef:, half:],
        acc[:n_coef, half:] + acc[n_coef:, :half],
    )


def dot_nn(a, b):
    return jnp.dot(a, b, preferred_element_type=F32)


def dot_nt(a, b):
    return lax.dot_general(a, b, (((1,), (1,)), ((), ())), preferred_element_type=F32)


def rotate_columns(
    peers, width, coef_ref, rot_ref, send_ref, clus_ref, crot_ref, pool_ref, sums_ref, out_refs, sel
):
    comps, n_coef, sph = coef_ref.shape
    rots = rot_ref.shape[0]
    pool = rots * sph
    members, each = sums_ref.shape[0], sums_ref.shape[1]
    group = members * each
    x_all = jnp.concatenate([coef_ref[x].astype(BF16) for x in range(comps)], axis=1)
    for r in range(rots):
        turned = dot_nn(rot_ref[r], x_all).astype(BF16)
        for x in range(comps):
            pool_ref[x * n_coef : (x + 1) * n_coef, r * sph : (r + 1) * sph] = turned[
                :, x * sph : (x + 1) * sph
            ]
    total = peers * width
    col_iota = lax.broadcasted_iota(jnp.int32, (total, sph), 1)
    clus_iota = lax.broadcasted_iota(jnp.int32, (group, sph), 0)
    for r in range(rots):
        hit = send_ref[...] == col_iota + r * sph
        sel[:total, r * sph : (r + 1) * sph] = jnp.where(hit, 1.0, 0.0).astype(BF16)
        own = (clus_ref[...] == clus_iota) & (crot_ref[...] == r)
        sel[total:, r * sph : (r + 1) * sph] = jnp.where(own, 1.0, 0.0).astype(BF16)
    rows = comps * n_coef
    step = 3 * sph
    for at in range(0, rows, step):
        picked = dot_nt(sel[...], pool_ref[at : at + step, :])
        for p in range(peers):
            out_refs[p][:, at : at + step] = picked[p * width : (p + 1) * width].astype(BF16)
        for q in range(members):
            row = total + q * each
            sums_ref[q, :, at : at + step] = picked[row : row + each]


def count_slots(peers, per_shell, sent_ref, pool_ref, inc_ref, pcol_ref, prot_ref, count_s, sel_s):
    sph = inc_ref.shape[2]
    shells = pcol_ref.shape[0] // per_shell
    pool = pool_ref.shape[1]
    total = peers * sent_ref.shape[1]
    q_iota = lax.broadcasted_iota(jnp.int32, (total, sph), 0) + pool
    rot_of = jnp.full((total, sph), -1.0, F32)
    for h in range(shells):
        count = jnp.zeros((total, sph), F32)
        for s in range(h * per_shell, (h + 1) * per_shell):
            hit = pcol_ref[s : s + 1, :] == q_iota
            count = count + jnp.where(hit, 1.0, 0.0)
            rot_of = jnp.where(hit, prot_ref[s : s + 1, :].astype(F32), rot_of)
        count_s[:, h * sph : (h + 1) * sph] = count.astype(BF16)
    rot_of = jnp.max(rot_of, axis=1, keepdims=True)
    j_iota = lax.broadcasted_iota(jnp.int32, (sph, sph), 0)
    for r in range(pool // sph):
        for h in range(shells):
            count = jnp.zeros((sph, sph), F32)
            for s in range(h * per_shell, (h + 1) * per_shell):
                count = count + jnp.where(pcol_ref[s : s + 1, :] == j_iota + r * sph, 1.0, 0.0)
            sel_s[r, :, h * sph : (h + 1) * sph] = count.astype(BF16)
    return rot_of


def gather_columns(
    peers, per_shell, rot_of, pool_ref, exp_ref, flat_ref, recv_refs,
    coup_ref, axial_ref, up_ref, far_ref, rott_ref, mie_ref, inc_ref,
    gid_ref, crot_ref, pcol_ref, out_ref,
    recv_s, count_s, sel_s, taken_s, far_s, gath_s,
):
    comps, n_coef, sph = inc_ref.shape
    dirs = comps // 2
    slots = pcol_ref.shape[0]
    shells = slots // per_shell
    pool = pool_ref.shape[1]
    rots = pool // sph
    width = recv_refs[0].shape[0]
    total = peers * width
    clus = coup_ref.shape[0]
    half = dirs * sph

    arrived = jnp.concatenate([recv_refs[p][...] for p in range(peers)], axis=0)
    recv_s[...] = arrived.T

    clus_iota = lax.broadcasted_iota(jnp.int32, (clus, sph), 0)
    n_mem, n_grp, each = exp_ref.shape[0], exp_ref.shape[1], exp_ref.shape[2]
    for a in range(n_mem):
        for b in range(n_grp):
            row = (a * n_grp + b) * each
            flat_ref[row : row + each, :] = exp_ref[a, b]
    member = jnp.where(gid_ref[...] == clus_iota, 1.0, 0.0).astype(F32)
    weights = jnp.dot(coup_ref[...], member, precision=lax.Precision.HIGHEST, preferred_element_type=F32)
    near_sum = jnp.dot(
        flat_ref[...].T, weights, precision=lax.Precision.HIGHEST, preferred_element_type=F32
    )
    folded = jnp.concatenate(
        [near_sum[x * n_coef : (x + 1) * n_coef] for x in range(comps)], axis=1
    )
    high = folded.astype(BF16)
    low = (folded - high.astype(F32)).astype(BF16)
    high_re, high_im = pair_apply(up_ref[...], high)
    low_re, low_im = pair_apply(up_ref[...], low)
    reached = jnp.concatenate([high_re + low_re, high_im + low_im], axis=1).astype(BF16)
    far_re, far_im = pair_apply(far_ref[...], reached)
    far_s[:, :half] = far_re
    far_s[:, half:] = far_im

    @pl.loop(0, rots)
    def _(r):
        first = pl.multiple_of(r * sph, sph)
        mine = rot_of == r.astype(F32)
        kept = jnp.where(mine, count_s[...].astype(F32), 0.0).astype(BF16)
        sel = jnp.concatenate([sel_s[r], kept], axis=0)
        for x in range(comps):
            rows = slice(x * n_coef, (x + 1) * n_coef)
            lhs = jnp.concatenate([pool_ref[rows, pl.ds(first, sph)], recv_s[rows, :]], axis=1)
            taken = dot_nn(lhs, sel).astype(BF16)
            for h in range(shells):
                taken_s[h, :, x * sph : (x + 1) * sph] = taken[:, h * sph : (h + 1) * sph]
        acc = dot_nn(axial_ref[0].reshape(2 * n_coef, n_coef), taken_s[0])
        for h in range(1, shells):
            acc = acc + dot_nn(axial_ref[h].reshape(2 * n_coef, n_coef), taken_s[h])
        moved_re, moved_im = pair_combine(acc, n_coef, half)
        here = jnp.concatenate([crot_ref[...]] * dirs, axis=1) == r
        gath_s[r, :, :half] = (moved_re + jnp.where(here, far_s[:, :half], 0.0)).astype(BF16)
        gath_s[r, :, half:] = (moved_im + jnp.where(here, far_s[:, half:], 0.0)).astype(BF16)

    field = dot_nn(rott_ref[...], gath_s[...].reshape(rots * n_coef, comps * sph))
    mie_r = mie_ref[:, 0:1]
    mie_i = mie_ref[:, 1:2]
    for d in range(dirs):
        re = inc_ref[d] + field[:, d * sph : (d + 1) * sph]
        im = inc_ref[dirs + d] + field[:, half + d * sph : half + (d + 1) * sph]
        out_ref[d] = mie_r * re - mie_i * im
        out_ref[dirs + d] = mie_r * im + mie_i * re


def on_device(
    coefficients,
    incident,
    mie_coeffs,
    rot_table,
    axial_shells,
    up_axial,
    far_axial,
    coupling,
    cluster_ids,
    center_rot,
    pair_col,
    pair_rot,
    send_col,
):
    comps, n_coef, sph = coefficients.shape
    rots = rot_table.shape[0]
    pool = rots * sph
    rows = comps * n_coef
    clus = coupling.shape[0]
    n_grp, n_mem = lax.axis_size("grp"), lax.axis_size("mem")
    group = clus // n_grp
    each = group // n_mem
    peers, width = send_col.shape
    total = peers * width
    shells = axial_shells.shape[0]
    per_shell = pair_col.shape[0] // shells
    vmem = pl.BlockSpec(memory_space=pltpu.VMEM)
    clus_row = cluster_ids.reshape(1, sph)
    crot_row = center_rot.reshape(1, sph)

    rott = jnp.transpose(rot_table, (2, 0, 1)).reshape(n_coef, rots * n_coef)
    eye = jnp.arange(clus)[:, None] == jnp.arange(clus)[None, :]
    coup_t = jnp.where(eye, F32(0.0), coupling).T
    coup_t = coup_t.reshape(n_grp, n_mem, each, clus).transpose(1, 0, 2, 3).reshape(clus, clus)
    gid = clus_row + lax.axis_index("grp") * group
    dma = pltpu.SemaphoreType.DMA
    return pl.pallas_call(
        functools.partial(sweep_kernel, peers, per_shell, n_grp, n_mem),
        out_shape=jax.ShapeDtypeStruct((comps, n_coef, sph), F32),
        in_specs=[vmem] * 15,
        out_specs=vmem,
        scratch_shapes=[
            pltpu.VMEM((rows, pool), BF16),
            pltpu.VMEM((n_mem, each, rows), F32),
            pltpu.VMEM((peers, width, rows), BF16),
            pltpu.VMEM((total + group, pool), BF16),
            pltpu.VMEM((peers, width, rows), BF16),
            pltpu.VMEM((n_mem, n_grp, each, rows), F32),
            pltpu.VMEM((clus, rows), F32),
            pltpu.VMEM((rows, total), BF16),
            pltpu.VMEM((total, shells * sph), BF16),
            pltpu.VMEM((rots, sph, shells * sph), BF16),
            pltpu.VMEM((shells, n_coef, comps * sph), BF16),
            pltpu.VMEM((n_coef, comps * sph), F32),
            pltpu.VMEM((rots, n_coef, comps * sph), BF16),
            pltpu.VMEM((n_mem - 1, each, rows), F32),
        ]
        + [dma((peers,))] * 2
        + [dma((n_mem - 1,))] * 2
        + [dma((n_grp - 1,))] * 2
        + [dma((n_mem - 1,))] * 2,
        compiler_params=pltpu.CompilerParams(
            collective_id=0, has_side_effects=True, vmem_limit_bytes=52 * MIB
        ),
        name="sweep",
    )(
        coefficients, rot_table, send_col.reshape(total, 1), clus_row,
        coup_t, axial_shells, up_axial, far_axial, rott, mie_coeffs.T, incident,
        gid, crot_row, pair_col, pair_rot,
    )


def solution(mesh):
    cut = ("grp", "mem")
    in_specs = (
        P(None, None, cut),
        P(None, None, cut),
        P(),
        P(),
        P(),
        P(),
        P(),
        P(),
        P(cut),
        P(cut),
        P(None, cut),
        P(None, cut),
        P(cut, None),
    )
    return jax.shard_map(
        on_device, mesh=mesh, in_specs=in_specs, out_specs=P(None, None, cut), check_vma=False
    )
```
